256 devices in a mesh: grp: 8 (over x, core), dev: 32 (over y, z).
Axes of the slice: x: 4, y: 4, z: 8, core: 2. Of those that a mesh axis runs over, the one named last changes fastest.
Arguments:
- q_latent: bfloat16 [4096, 1536], P(('grp', 'dev')), parts along dimension 0, may hold values from -51 to 51
- w_uq: bfloat16 [1536, 12288], P(None, 'dev'), may hold values from -0.15625 to 0.15625
- w_kup: bfloat16 [8192, 512], P('dev'), may hold values from -0.25 to 0.25
- w_vup: bfloat16 [512, 8192], P(None, 'dev'), may hold values from -0.25 to 0.25
- prefix_keys: bfloat16 [32768, 8192], P('grp', 'dev'), parts along dimension 0, may hold values from -6 to 6
- prefix_values: bfloat16 [32768, 8192], P('grp', 'dev'), parts along dimension 0, may hold values from -6 to 6
- prefix_rope: bfloat16 [64, 32768], P(None, 'grp'), parts along dimension 1, may hold values from -6 to 6
- private_cache: bfloat16 [4096, 384, 576], P(('grp', 'dev')), parts along dimension 0, may hold values from -6 to 6
- lengths: int32 [4096], P(('grp', 'dev')), parts along dimension 0, may hold values from 1 to 384, 98304 in all
- prefix_len: int32 [8], P('grp'), parts along dimension 0, may hold values from 2048 to 4096
Outputs:
- attn: bfloat16 [4096, 8192], P('grp', 'dev'), parts along dimension 0
The draws below stay inside these ranges and needn't reach their ends.
There are 8 independent parts, one for each index of `grp`. The reference program is written for one: setup_inputs(seed, part) draws one part's arguments, and reference() takes and returns one part's arrays. A program takes and returns all parts, laid end to end along the dimension named above; an argument that names none is the same for every part. Nothing has to cross between parts.
Inputs may be any that keep to these rules, and one draw needn't show every extreme that they name: Within each group the lengths sum to 98304.
All inputs are finite; a program needn't handle non-finite values.
Results may differ from the reference program's by a relative error of at most 0.04.
Values may be sent and summed in bfloat16 or wider, within the bound.
A program may use at most 128 MiB of HBM per device.

```python
import math
import jax
import jax.numpy as jnp
import numpy as np
from jax import lax

H = 64
QL = 1536
KVL = 512
NOPE = 128
ROPE = 64
VD = 128
PREFIX = 4096
PRIV = 384
REQ = 512


def draw_q_latent(key, part):
    key = jax.random.fold_in(key, 3)
    return jnp.clip(jax.random.normal(key, (REQ, QL), jnp.float32), -6.0, 6.0).astype(jnp.bfloat16)


def draw_prefix_len(key, part):
    key = jax.random.fold_in(key, 7)
    pick_key, middle_key = jax.random.split(key)
    pick = jax.random.randint(pick_key, (1,), 0, 2).astype(jnp.int32)
    middle = jax.random.randint(middle_key, (1,), PREFIX // 2, PREFIX + 1).astype(jnp.int32)
    longest = jnp.full((1,), PREFIX, jnp.int32)
    return jnp.where(pick == 0, longest, middle).astype(jnp.int32)


def steps_of(rng, shape, pieces, low, high):
    gain = 1.0
    for position, shards_of in pieces:
        draws = jax.random.uniform(jax.random.fold_in(jax.random.fold_in(rng, 6), position), (shards_of,), jnp.float32, low / len(pieces), high / len(pieces))
        gain = gain * jnp.repeat(jnp.exp(draws), shape[position] // shards_of).reshape((-1,) + (1,) * (len(shape) - 1 - position))
    return gain


def profile(number_of, total, bound, slope):
    weights = [(1 << 20) // math.isqrt(grade ** slope) + 1 for grade in range(2, number_of + 1)]
    spare, given = total - bound - (number_of - 1), [1] * (number_of - 1)
    while spare > 0:
        movable = [i for i in range(number_of - 1) if given[i] < bound]
        mass, left = sum([weights[i] for i in movable]), spare
        for i in movable:
            more = min(bound - given[i], max(1, left * weights[i] // mass), spare)
            given[i] = given[i] + more
            spare = spare - more
    return np.array([bound] + given)


def ragged(stream_key, amount, total, most, lean):
    if amount == 2:
        one = jax.random.randint(stream_key, (), max(1, total - most), min(most, total - 1) + 1)
        return jnp.stack([one, total - one])
    sizes = jnp.asarray(profile(amount, total, most, lean), jnp.int32)
    pairs = (amount - 1) // 2
    giver, sink = sizes[1:1 + 2 * pairs:2], sizes[2:2 + 2 * pairs:2]
    margin = jnp.minimum(giver - 1, most - sink)
    shifted = jax.random.randint(jax.random.fold_in(stream_key, 1), (pairs,), 0, 1 << 20) % (margin + 1)
    sizes = sizes.at[1:1 + 2 * pairs:2].set(giver - shifted).at[2:2 + 2 * pairs:2].set(sink + shifted)
    return sizes[jax.random.permutation(jax.random.fold_in(stream_key, 2), amount)]


def gaussian(key, dims, spread, most, cuts=(), dtype=jnp.bfloat16):
    level = steps_of(key, dims, cuts, -0.22, 0.18) if cuts else 1.0
    values = jax.random.normal(key, dims, jnp.float32) * spread * level
    return jnp.minimum(jnp.maximum(values, -most), most).astype(dtype)


def setup_inputs(seed: int = 0, part: int = 0) -> dict:
    splits = jax.random.split(jax.random.key(seed), 11)
    part_splits = jax.random.split(jax.random.fold_in(splits[10], part), 11)
    q_latent = draw_q_latent(jax.random.fold_in(jax.random.fold_in(splits[10], part), 71), part)
    w_uq = gaussian(splits[1], (QL, H * (NOPE + ROPE)), QL ** -0.5, 0.15625, ((1, 32),))
    w_kup = gaussian(splits[2], (H * NOPE, KVL), KVL ** -0.5, 0.25, ((0, 32),))
    w_vup = gaussian(splits[3], (KVL, H * VD), KVL ** -0.5, 0.25, ((1, 32),))
    prefix_keys = gaussian(part_splits[4], (PREFIX, H * NOPE), 1.0, 6.0, ((1, 32),))
    prefix_values = gaussian(part_splits[5], (PREFIX, H * VD), 1.0, 6.0, ((1, 32),))
    prefix_rope = gaussian(part_splits[6], (ROPE, PREFIX), 1.0, 6.0)
    private_cache = gaussian(part_splits[7], (REQ, PRIV, KVL + ROPE), 1.0, 6.0, ((0, 32),))
    lengths = ragged(part_splits[8], REQ, REQ * PRIV // 2, PRIV, 2).astype(jnp.int32)
    prefix_len = draw_prefix_len(jax.random.fold_in(jax.random.fold_in(splits[10], part), 71), part)
    return dict(q_latent=q_latent, w_uq=w_uq, w_kup=w_kup, w_vup=w_vup, prefix_keys=prefix_keys, prefix_values=prefix_values, prefix_rope=prefix_rope, private_cache=private_cache, lengths=lengths, prefix_len=prefix_len)


def reference(q_latent, w_uq, w_kup, w_vup, prefix_keys, prefix_values, prefix_rope, private_cache, lengths, prefix_len):
    total = q_latent.shape[0]
    scale = 1.0 / math.sqrt(NOPE + ROPE)
    q_full = jnp.dot(q_latent, w_uq, preferred_element_type=jnp.float32).astype(jnp.bfloat16)
    q_full = q_full.reshape(total, H, NOPE + ROPE)
    q_nope = q_full[:, :, :NOPE]
    q_rope = q_full[:, :, NOPE:]
    kup_heads = w_kup.reshape(H, NOPE, KVL)
    absorbed = jnp.einsum('rhn,hnc->rhc', q_nope.astype(jnp.float32), kup_heads.astype(jnp.float32)).astype(jnp.bfloat16)
    q_abs = jnp.concatenate([absorbed, q_rope], axis=2)

    def private_one(packed):
        query, cache, live = packed
        scores = jnp.dot(query, cache.T, preferred_element_type=jnp.float32) * scale
        mask = jnp.arange(PRIV)[None, :] < live
        scores = jnp.where(mask, scores, -jnp.inf)
        top = lax.optimization_barrier(jnp.max(scores, axis=1, keepdims=True))
        expo = jnp.exp(scores - top)
        denom = lax.optimization_barrier(jnp.sum(expo, axis=1))
        weights = expo.astype(jnp.bfloat16)
        latent = jnp.dot(weights, cache[:, :KVL], preferred_element_type=jnp.float32)
        latent = (latent / denom[:, None]).astype(jnp.bfloat16)
        return (latent, top[:, 0] + jnp.log(denom))
    latent_out, private_lse = lax.map(private_one, (q_abs, private_cache, lengths))
    latent_heads = jnp.transpose(latent_out, (1, 0, 2))
    lse_heads = jnp.transpose(private_lse, (1, 0))
    nope_heads = jnp.transpose(q_nope, (1, 0, 2))
    rope_heads = jnp.transpose(q_rope, (1, 0, 2))
    key_heads = jnp.transpose(prefix_keys.reshape(PREFIX, H, NOPE), (1, 0, 2))
    value_heads = jnp.transpose(prefix_values.reshape(PREFIX, H, VD), (1, 0, 2))
    vup_heads = jnp.transpose(w_vup.reshape(KVL, H, VD), (1, 0, 2))
    live_prefix = prefix_len[0]

    def head_one(packed):
        qn, qr, keys, values, latent, lse_v, vup = packed
        scores = jnp.dot(qn, keys.T, preferred_element_type=jnp.float32) + jnp.dot(qr, prefix_rope, preferred_element_type=jnp.float32)
        scores = scores * scale
        mask = jnp.arange(PREFIX)[None, :] < live_prefix
        scores = jnp.where(mask, scores, -jnp.inf)
        top = lax.optimization_barrier(jnp.max(scores, axis=1, keepdims=True))
        expo = jnp.exp(scores - top)
        denom = lax.optimization_barrier(jnp.sum(expo, axis=1))
        weights = expo.astype(jnp.bfloat16)
        prefix_out = jnp.dot(weights, values, preferred_element_type=jnp.float32) / denom[:, None]
        lse_p = top[:, 0] + jnp.log(denom)
        private_out = jnp.dot(latent, vup, preferred_element_type=jnp.float32)
        upper = jnp.maximum(lse_p, lse_v)
        first = jnp.exp(lse_p - upper)[:, None]
        second = jnp.exp(lse_v - upper)[:, None]
        return (first * prefix_out + second * private_out) / (first + second)
    merged = lax.map(head_one, (nope_heads, rope_heads, key_heads, value_heads, latent_heads, lse_heads, vup_heads))
    return jnp.transpose(merged, (1, 0, 2)).reshape(total, H * VD).astype(jnp.bfloat16)
```

```python
import math

import jax
import jax.numpy as jnp
from jax import lax
from jax.experimental import pallas as pl
from jax.experimental.pallas import tpu as pltpu
from jax.sharding import PartitionSpec as P

KVL = 512
NOPE = 128
ROPE = 64
VD = 128
MESH = pl.DeviceIdType.MESH
NY, NZ, NX = 4, 8, 4
RQ = 16
SLOTS = 384
PREFIX = 4096
QL = 1536
TB = 512
SCALE2 = math.log2(math.e) / math.sqrt(NOPE + ROPE)
F32 = jnp.float32
BF16 = jnp.bfloat16


def nn(a, b):
    return lax.dot_general(a, b, (((1,), (0,)), ((), ())), preferred_element_type=F32)


def nt(a, b):
    return lax.dot_general(a, b, (((1,), (1,)), ((), ())), preferred_element_type=F32)


def near(i):
    odd = lax.rem(i, 2)
    return odd * lax.div(i + 1, 2) + (1 - odd) * (NZ - lax.div(i, 2))


def each(low, high, step):
    def one(i, carry):
        step(i)
        return carry

    lax.fori_loop(low, high, one, 0)


def kernel(
    ql, wuq, wkup, wvup, keys_h, vals_h, rope_h, cache_h, lens, plen, out,
    wuq_v, wp, keys, vals, rope, cache, ag, qb, zq, wk, wv, absb, rps, rec1, rec1r,
    qf, qrf, lf, lse, send2, rec2, recl, outz, mbuf, recz, recm, sc, po, plse,
    ld, agz_s, agz_r, yp_s, yp_r, ym_s, ym_r, f_s, f_r, qz_s, qz_r,
    kz_s, kz_r, kx_s, kx_r, kc_s, kc_r, vz_s, vz_r, vx_s, vx_r, vc_s, vc_r,
    a_s, a_r, ar_s, ar_r, b_s, b_r, bl_s, bl_r, c_s, c_r, cm_s, cm_r,
):
    g = lax.axis_index("grp")
    d = lax.axis_index("dev")
    x, c = lax.div(g, 2), lax.rem(g, 2)
    y, z = lax.div(d, NZ), lax.rem(d, NZ)

    def yat(k):
        return lax.rem(y + (k + NY), NY)

    def zat(k):
        return lax.rem(z + (k + NZ), NZ)

    def to_y(k):
        return (g, yat(k) * NZ + z)

    def to_z(k):
        return (g, y * NZ + zat(k))

    def to_x(k):
        return (lax.rem(x + k, NX) * 2 + c, d)

    twin = (x * 2 + 1 - c, d)
    sends = []

    def copy(src, dst, ss, rs, dev):
        return pltpu.make_async_remote_copy(
            src_ref=src, dst_ref=dst, send_sem=ss, recv_sem=rs, device_id=dev, device_id_type=MESH
        )

    def push(*what):
        one = copy(*what)
        one.start()
        sends.append(one.wait_send)

    def push_near(what):
        each(1, NZ, lambda i: what(near(i)).start())
        sends.append(lambda: each(1, NZ, lambda i: what(i).wait_send()))

    def push_x(what):
        each(1, NX, lambda i: what(i).start())
        sends.append(lambda: each(1, NX, lambda i: what(i).wait_send()))

    def landed(dst, ss, rs):
        pltpu.make_async_remote_copy(
            src_ref=dst, dst_ref=dst, send_sem=ss, recv_sem=rs, device_id=twin, device_id_type=MESH
        ).wait_recv()

    krow = pl.multiple_of(c * 128 + x * 32, 32)
    vrow = pl.multiple_of(x * 128, 128)
    vcol = pl.multiple_of(c * 128, 128)
    ccol = pl.multiple_of((1 - c) * 128, 128)

    loads = [
        pltpu.make_async_copy(ql, ag.at[y, z], ld.at[0]),
        pltpu.make_async_copy(wuq, wuq_v, ld.at[1]),
        pltpu.make_async_copy(wkup.at[pl.ds(krow, 32), :], wk.at[z, pl.ds(krow, 32), :], ld.at[2]),
        pltpu.make_async_copy(
            wvup.at[pl.ds(vrow, 128), pl.ds(vcol, 128)],
            wv.at[z, c, pl.ds(vrow, 128), :],
            ld.at[3],
        ),
        pltpu.make_async_copy(keys_h, keys, ld.at[4]),
        pltpu.make_async_copy(rope_h, rope, ld.at[5]),
        pltpu.make_async_copy(vals_h, vals, ld.at[6]),
        pltpu.make_async_copy(cache_h, cache, ld.at[7]),
    ]
    for load in loads:
        load.start()

    barrier = pltpu.get_barrier_semaphore()

    def greet(dev):
        pl.semaphore_signal(barrier, inc=1, device_id=dev, device_id_type=MESH)

    each(1, NZ, lambda k: greet(to_z(k)))
    each(1, NY, lambda k: greet(to_y(k)))
    each(1, NX, lambda k: greet(to_x(k)))
    greet(twin)
    pl.semaphore_wait(barrier, NZ + NY + NX - 2)

    def own(k):
        return copy(ql, ag.at[y, z], agz_s.at[k], agz_r.at[k], to_z(k))

    def beside(k, up):
        block = ag.at[y, zat(-k)]
        if up:
            return copy(block, block, yp_s.at[k], yp_r.at[k], to_y(1))
        return copy(block, block, ym_s.at[k], ym_r.at[k], to_y(3))

    loads[0].wait()
    push_near(own)
    beside(0, True).start()
    beside(0, False).start()
    sends.append(lambda: each(0, NZ, lambda k: beside(k, True).wait_send()))
    sends.append(lambda: each(0, NZ, lambda k: beside(k, False).wait_send()))

    loads[1].wait()

    def permute(i, _):
        rows = pl.ds(pl.multiple_of(i * 256, 256), 256)
        w = wuq_v[rows, :]
        wp[rows, 0:128] = w[:, 0:128]
        wp[rows, 128:256] = w[:, 192:320]
        wp[rows, 256:384] = jnp.concatenate([w[:, 128:192], w[:, 320:384]], axis=1)
        return 0

    lax.fori_loop(0, QL // 256, permute, 0)

    def handed(i):
        k = near(i)
        landed(ag.at[y, zat(-k)], agz_s.at[k], agz_r.at[k])
        beside(k, True).start()
        beside(k, False).start()

    each(1, NZ, handed)

    push_near(
        lambda k: copy(
            wkup.at[pl.ds(krow, 32), :],
            wk.at[z, pl.ds(krow, 32), :],
            kz_s.at[k],
            kz_r.at[k],
            to_z(k),
        )
    )

    def queries(k):
        yy = yat(k)
        q = nn(ag[yy].reshape(NZ * RQ, QL), wp[...]).astype(BF16)
        qb[yy] = q.reshape(NZ, RQ, 384)
        zq[z, yy] = qb[yy, z]
        push_near(
            lambda j: copy(
                qb.at[yy, zat(j)], zq.at[z, yy], qz_s.at[k, j], qz_r.at[k, j], to_z(j)
            )
        )

    queries(0)

    def relay(k, up):
        block = ag.at[yat(-1 if up else 1), zat(-k)]
        return copy(block, block, f_s.at[k], f_r.at[k], to_y(1 if up else 3))

    def rows_beside(k, up):
        zs = zat(-k)
        landed(ag.at[yat(-1), zs], yp_s.at[k], yp_r.at[k])
        landed(ag.at[yat(1), zs], ym_s.at[k], ym_r.at[k])
        relay(k, up).start()

    def pair(k):
        rows_beside(k, False)
        rows_beside(NZ - k, True)

    rows_beside(0, True)
    each(1, NZ // 2, pair)
    rows_beside(NZ // 2, False)
    sends.append(lambda: each(0, NZ, lambda k: relay(k, True).wait_send()))

    queries(1)
    queries(3)

    loads[2].wait()
    each(
        1,
        NZ,
        lambda k: landed(wk.at[zat(-k), pl.ds(krow, 32), :], kz_s.at[k], kz_r.at[k]),
    )

    def wk_x(k):
        block = wk.at[:, pl.ds(krow, 32), :]
        return copy(block, block, kx_s.at[k], kx_r.at[k], to_x(k))

    push_x(wk_x)

    live = plen[0]

    def prefix(k, h):
        yy = yat(k)
        hc = slice(h * 128, (h + 1) * 128)
        q = qb[yy].reshape(NZ * RQ, 384)
        qn = q[:, hc]
        qr = q[:, 256 + h * ROPE : 256 + (h + 1) * ROPE]

        def score(t, m):
            t0 = pl.multiple_of(t * TB, TB)
            s = nt(qn, keys[pl.ds(t0, TB), hc]) + nn(qr, rope[:, pl.ds(t0, TB)])
            col = t0 + lax.broadcasted_iota(jnp.int32, s.shape, 1)
            s = jnp.where(col < live, s * SCALE2, -jnp.inf)
            sc[:, pl.ds(t0, TB)] = s
            for j in range(TB // 128):
                m = jnp.maximum(m, s[:, j * 128 : (j + 1) * 128])
            return m

        m = lax.fori_loop(0, PREFIX // TB, score, jnp.full((128, 128), -jnp.inf, F32))
        top = jnp.max(m, axis=1, keepdims=True)

        def weigh(t, carry):
            acc, den = carry
            t0 = pl.multiple_of(t * TB, TB)
            p = jnp.exp2(sc[:, pl.ds(t0, TB)] - top)
            for j in range(TB // 128):
                den = den + p[:, j * 128 : (j + 1) * 128]
            return acc + nn(p.astype(BF16), vals[pl.ds(t0, TB), hc]), den

        zero = jnp.zeros((128, 128), F32)
        acc, den = lax.fori_loop(0, PREFIX // TB, weigh, (zero, zero))
        den = jnp.sum(den, axis=1, keepdims=True)
        po[h, yy] = (acc / den).reshape(NZ, RQ, VD)
        lse2 = jnp.broadcast_to(top + jnp.log(den) * math.log2(math.e), (128, 128))
        plse[h, yy] = lse2.reshape(NZ, RQ, 128)

    loads[4].wait()
    loads[5].wait()
    loads[6].wait()
    prefix(0, 0)

    each(0, NZ, lambda k: landed(ag.at[yat(2), zat(-k)], f_s.at[k], f_r.at[k]))
    queries(2)

    push_near(
        lambda k: copy(
            wvup.at[pl.ds(vrow, 128), pl.ds(vcol, 128)],
            wv.at[z, c, pl.ds(vrow, 128), :],
            vz_s.at[k],
            vz_r.at[k],
            to_z(k),
        )
    )

    prefix(0, 1)

    def wk_landed(k):
        rows = pl.ds(pl.multiple_of(c * 128 + lax.rem(x - k + NX, NX) * 32, 32), 32)
        landed(wk.at[:, rows, :], kx_s.at[k], kx_r.at[k])

    each(1, NX, wk_landed)
    half = wk.at[:, pl.ds(vcol, 128), :]
    push(half, half, kc_s.at[0], kc_r.at[0], twin)

    def arrive(k):
        each(1, NZ, lambda j: landed(zq.at[zat(-j), yat(k)], qz_s.at[k, j], qz_r.at[k, j]))

    def absorb(ks):
        def one(zz, _):
            q = jnp.concatenate([zq[zz, yat(k)] for k in ks], axis=0)
            rows = pl.ds(pl.multiple_of(zz * RQ, RQ), RQ)
            for h in range(2):
                hc = slice(h * 128, (h + 1) * 128)
                a = nn(q[:, hc], wk[zz, hc, :]).astype(BF16)
                for i, k in enumerate(ks):
                    absb[yat(k), h, rows, :] = a[i * RQ : (i + 1) * RQ]
            for i, k in enumerate(ks):
                rps[yat(k), rows, :] = q[i * RQ : (i + 1) * RQ, 256:384]
            return 0

        lax.fori_loop(0, NZ, one, 0)
        for k in ks:
            if k:
                yy = yat(k)
                push(absb.at[yy], rec1.at[y], a_s.at[k], a_r.at[k], to_y(k))
                push(rps.at[yy], rec1r.at[y], ar_s.at[k], ar_r.at[k], to_y(k))

    arrive(1)
    arrive(3)
    landed(wk.at[:, pl.ds(ccol, 128), :], kc_s.at[0], kc_r.at[0])
    absorb((1, 3))
    arrive(0)
    arrive(2)
    absorb((2, 0))

    loads[3].wait()
    each(
        1,
        NZ,
        lambda k: landed(wv.at[zat(-k), c, pl.ds(vrow, 128), :], vz_s.at[k], vz_r.at[k]),
    )

    def wv_x(k):
        block = wv.at[:, c, pl.ds(vrow, 128), :]
        return copy(block, block, vx_s.at[k], vx_r.at[k], to_x(k))

    push_x(wv_x)


    def spread(k, src, srcr):
        yy = yat(k)
        for h in range(2):
            rows = pl.ds(pl.multiple_of(h * 512 + yy * 128, 128), 128)
            for j in range(4):
                qf[j, rows, :] = src[h, :, j * 128 : (j + 1) * 128].astype(F32)
        qrf[pl.ds(pl.multiple_of(yy * 128, 128), 128), :] = srcr[...].astype(F32)

    spread(0, absb.at[y], rps.at[y])
    prefix(1, 0)
    prefix(1, 1)
    prefix(3, 0)
    prefix(3, 1)


    def wv_landed(k):
        rows = pl.ds(pl.multiple_of(lax.rem(x - k + NX, NX) * 128, 128), 128)
        landed(wv.at[:, c, rows, :], vx_s.at[k], vx_r.at[k])

    each(1, NX, wv_landed)
    half = wv.at[:, c]
    push(half, half, vc_s.at[0], vc_r.at[0], twin)

    loads[7].wait()
    for k in range(1, NY):
        yy = yat(-k)
        landed(rec1.at[yy], a_s.at[k], a_r.at[k])
        landed(rec1r.at[yy], ar_s.at[k], ar_r.at[k])
        spread(-k, rec1.at[yy], rec1r.at[yy])

    lse[...] = jnp.zeros_like(lse)

    def private(r, _):
        q = jnp.concatenate([qf[j, pl.ds(r, 64, stride=RQ), :] for j in range(4)], axis=1)
        q = q.astype(BF16)
        qr = qrf[pl.ds(r, 32, stride=RQ), :]
        qr = jnp.concatenate([qr[:, :ROPE], qr[:, ROPE:]], axis=0).astype(BF16)
        s = nn(q, cache[r, :KVL, :]) + nn(qr, cache[r, KVL:, :])
        col = lax.broadcasted_iota(jnp.int32, s.shape, 1)
        s = jnp.where(col < lens[r], s * SCALE2, -jnp.inf)
        top = jnp.max(s, axis=1, keepdims=True)
        p = jnp.exp2(s - top)
        den = jnp.sum(p, axis=1, keepdims=True)
        latent = nt(p.astype(BF16), cache[r, :KVL, :]) / den
        for j in range(4):
            lf[j, pl.ds(r, 64, stride=RQ), :] = latent[:, j * 128 : (j + 1) * 128]
        lse2 = (top + jnp.log(den) * math.log2(math.e)).reshape(2, NY, NZ, 1)
        lane = lax.broadcasted_iota(jnp.int32, lse.shape, 3)
        lse[...] = jnp.where(lane == r, lse2, lse[...])
        return 0

    lax.fori_loop(0, RQ, private, 0, unroll=2)

    def gather(k, dst):
        yy = yat(k)
        for h in range(2):
            rows = pl.ds(pl.multiple_of(h * 512 + yy * 128, 128), 128)
            for j in range(4):
                dst[h, :, j * 128 : (j + 1) * 128] = lf[j, rows, :].astype(BF16)

    for k in (2, 1, 3):
        yy = yat(k)
        gather(k, send2.at[yy])
        push(send2.at[yy], rec2.at[y], b_s.at[k], b_r.at[k], to_y(k))
        push(lse.at[:, yy], recl.at[y], bl_s.at[k], bl_r.at[k], to_y(k))
    gather(0, rec2.at[y])
    recl[y] = lse[:, y]

    prefix(2, 0)
    prefix(2, 1)

    landed(wv.at[:, 1 - c], vc_s.at[0], vc_r.at[0])
    for k in range(1, NY):
        landed(recl.at[yat(-k)], bl_s.at[k], bl_r.at[k])
        landed(rec2.at[yat(-k)], b_s.at[k], b_r.at[k])
    total = recl[0]
    total = total.reshape(16, 128)
    for yy in range(1, NY):
        total = total + pltpu.roll(recl[yy].reshape(16, 128), yy * RQ, 1)
    mbuf[...] = total
    recm[z] = total
    push_near(lambda k: copy(mbuf, recm.at[z], cm_s.at[k], cm_r.at[k], to_z(k)))

    def project(zz, dst):
        rows = pl.ds(pl.multiple_of(zz * RQ, RQ), RQ)
        for h in range(2):
            lat = jnp.concatenate([rec2[yy, h, rows, :] for yy in range(NY)], axis=0)
            dst[zz, h] = nn(lat, wv[zz, h]).astype(BF16)

    def heads(k):
        return copy(outz.at[zat(k)], recz.at[z], c_s.at[k], c_r.at[k], to_z(k))

    def give(i):
        k = near(NZ - i)
        project(zat(k), outz)
        heads(k).start()

    each(1, NZ, give)
    sends.append(lambda: each(1, NZ, lambda k: heads(k).wait_send()))
    project(z, recz)

    def merge(zz):
        diag = lax.broadcasted_iota(jnp.int32, (64, 128), 0) == lax.broadcasted_iota(
            jnp.int32, (64, 128), 1
        )
        for h in range(2):
            row = jnp.broadcast_to(recm[zz, pl.ds(h * NZ + z, 1), :], (64, 128))
            plane = jnp.sum(jnp.where(diag, row, 0.0), axis=1, keepdims=True)
            mine = jnp.concatenate([po[h, yy, zz] for yy in range(NY)], axis=0)
            mine_lse = jnp.concatenate([plse[h, yy, zz] for yy in range(NY)], axis=0)
            upper = jnp.maximum(mine_lse, plane)
            first = jnp.exp2(mine_lse - upper)
            second = jnp.exp2(plane - upper)
            theirs = recz[zz, h].astype(F32)
            merged = ((first * mine + second * theirs) / (first + second)).astype(BF16)
            for yy in range(NY):
                rows = pl.ds(pl.multiple_of(yy * 128 + zz * RQ, RQ), RQ)
                out[rows, h * 128 : (h + 1) * 128] = merged[yy * RQ : (yy + 1) * RQ]

    def finish(i):
        k = near(i)
        zz = zat(-k)
        landed(recm.at[zz], cm_s.at[k], cm_r.at[k])
        landed(recz.at[zz], c_s.at[k], c_r.at[k])
        merge(zz)

    merge(z)
    each(1, NZ, finish)
    for wait in sends:
        wait()


def body(
    q_latent,
    w_uq,
    w_kup,
    w_vup,
    prefix_keys,
    prefix_values,
    prefix_rope,
    private_cache,
    lengths,
    prefix_len,
):
    cache = jnp.transpose(private_cache, (0, 2, 1))
    vm = pltpu.VMEM
    dma = pltpu.SemaphoreType.DMA
    hbm = pl.BlockSpec(memory_space=pl.ANY)
    smem = pl.BlockSpec(memory_space=pltpu.SMEM)
    scratch = [
        vm((QL, 384), BF16),
        vm((QL, 384), BF16),
        vm((PREFIX, 256), BF16),
        vm((PREFIX, 256), BF16),
        vm((ROPE, PREFIX), BF16),
        vm((RQ, KVL + ROPE, SLOTS), BF16),
        vm((NY, NZ, RQ, QL), BF16),
        vm((NY, NZ, RQ, 384), BF16),
        vm((NZ, NY, RQ, 384), BF16),
        vm((NZ, 256, KVL), BF16),
        vm((NZ, 2, KVL, VD), BF16),
        vm((NY, 2, NZ * RQ, KVL), BF16),
        vm((NY, NZ * RQ, 128), BF16),
        vm((NY, 2, NZ * RQ, KVL), BF16),
        vm((NY, NZ * RQ, 128), BF16),
        vm((4, 1024, 128), F32),
        vm((512, 128), F32),
        vm((4, 1024, 128), F32),
        vm((2, NY, NZ, 128), F32),
        vm((NY, 2, NZ * RQ, KVL), BF16),
        vm((NY, 2, NZ * RQ, KVL), BF16),
        vm((NY, 2, NZ, 128), F32),
        vm((NZ, 2, 64, VD), BF16),
        vm((16, 128), F32),
        vm((NZ, 2, 64, VD), BF16),
        vm((NZ, 16, 128), F32),
        vm((128, PREFIX), F32),
        vm((2, NY, NZ, RQ, VD), F32),
        vm((2, NY, NZ, RQ, 128), F32),
        dma((8,)),
    ]
    sems = [8, 8, 8, 8, 8, 8, 8, 8, (4, 8), (4, 8), 8, 8, 4, 4, 1, 1, 8, 8, 4, 4, 1, 1]
    sems += [4] * 8 + [8] * 4
    scratch += [dma(n if isinstance(n, tuple) else (n,)) for n in sems]
    return pl.pallas_call(
        kernel,
        out_shape=jax.ShapeDtypeStruct((512, 256), BF16),
        in_specs=[hbm] * 8 + [smem] * 2,
        out_specs=pl.BlockSpec(memory_space=vm),
        scratch_shapes=scratch,
        compiler_params=pltpu.CompilerParams(
            collective_id=0, has_side_effects=True, vmem_limit_bytes=58 * 2**20
        ),
        cost_estimate=pl.CostEstimate(
            flops=5 * 10**9, bytes_accessed=14 * 10**6, transcendentals=5 * 10**6
        ),
        name="latent_attention",
    )(
        q_latent, w_uq, w_kup, w_vup, prefix_keys, prefix_values, prefix_rope, cache, lengths,
        prefix_len,
    )


def solution(mesh):
    placed = (
        P(("grp", "dev"), None),
        P(None, "dev"),
        P("dev", None),
        P(None, "dev"),
        P("grp", "dev"),
        P("grp", "dev"),
        P(None, "grp"),
        P(("grp", "dev"), None, None),
        P(("grp", "dev")),
        P("grp"),
    )
    return jax.shard_map(
        body, mesh=mesh, in_specs=placed, out_specs=P("grp", "dev"), check_vma=False
    )
```

```python
import math

import jax
import jax.numpy as jnp
from jax import lax
from jax.experimental import pallas as pl
from jax.experimental.pallas import tpu as pltpu
from jax.sharding import PartitionSpec as P

KVL = 512
NOPE = 128
ROPE = 64
VD = 128
MESH = pl.DeviceIdType.MESH
NY, NZ, NX = 4, 8, 4
RQ = 16
RH = 8
SLOTS = 384
PREFIX = 4096
QL = 1536
TB = 512
SCALE2 = math.log2(math.e) / math.sqrt(NOPE + ROPE)
F32 = jnp.float32
BF16 = jnp.bfloat16


def nn(a, b):
    return lax.dot_general(a, b, (((1,), (0,)), ((), ())), preferred_element_type=F32)


def nt(a, b):
    return lax.dot_general(a, b, (((1,), (1,)), ((), ())), preferred_element_type=F32)


def near(i):
    odd = lax.rem(i, 2)
    return odd * lax.div(i + 1, 2) + (1 - odd) * (NZ - lax.div(i, 2))


def each(low, high, step):
    def one(i, carry):
        step(i)
        return carry

    lax.fori_loop(low, high, one, 0)


def kernel(
    ql, wuq, wkup, wvup, keys_h, vals_h, rope_h, cache_h, lens, plen, out,
    wuq_v, wp, keys, vals, rope, cache, ag, qb, zq, wk, wv, absb, rps, rec1, rec1r,
    qf, qrf, lf, lse, send2, rec2, recl, outz, mbuf, recz, recm, half0, sc, po, plse,
    ld, agz_s, agz_r, yp_s, yp_r, ym_s, ym_r, f_s, f_r, qz_s, qz_r,
    kz_s, kz_r, kc_s, kc_r, vz_s, vz_r, vx_s, vx_r, vc_s, vc_r,
    a_s, a_r, ar_s, ar_r, b_s, b_r, bl_s, bl_r, c_s, c_r, cm_s, cm_r,
):
    g = lax.axis_index("grp")
    d = lax.axis_index("dev")
    x, c = lax.div(g, 2), lax.rem(g, 2)
    y, z = lax.div(d, NZ), lax.rem(d, NZ)

    def yat(k):
        return lax.rem(y + (k + NY), NY)

    def zat(k):
        return lax.rem(z + (k + NZ), NZ)

    def to_y(k):
        return (g, yat(k) * NZ + z)

    def to_z(k):
        return (g, y * NZ + zat(k))

    def to_x(k):
        return (lax.rem(x + k, NX) * 2 + c, d)

    twin = (x * 2 + 1 - c, d)
    sends = []

    def copy(src, dst, ss, rs, dev):
        return pltpu.make_async_remote_copy(
            src_ref=src, dst_ref=dst, send_sem=ss, recv_sem=rs, device_id=dev, device_id_type=MESH
        )

    def push(*what):
        one = copy(*what)
        one.start()
        sends.append(one.wait_send)

    def push_near(what):
        each(1, NZ, lambda i: what(near(i)).start())
        sends.append(lambda: each(1, NZ, lambda i: what(i).wait_send()))

    def push_x(what):
        each(1, NX, lambda i: what(i).start())
        sends.append(lambda: each(1, NX, lambda i: what(i).wait_send()))

    def landed(dst, ss, rs):
        pltpu.make_async_remote_copy(
            src_ref=dst, dst_ref=dst, send_sem=ss, recv_sem=rs, device_id=twin, device_id_type=MESH
        ).wait_recv()

    vrow = pl.multiple_of(x * 128, 128)
    vcol = pl.multiple_of(c * 128, 128)
    ccol = pl.multiple_of((1 - c) * 128, 128)

    loads = [
        pltpu.make_async_copy(ql, ag.at[y, z], ld.at[0]),
        pltpu.make_async_copy(wuq, wuq_v, ld.at[1]),
        pltpu.make_async_copy(wkup.at[pl.ds(vcol, 128), :], wk.at[z, pl.ds(vcol, 128), :], ld.at[2]),
        pltpu.make_async_copy(
            wvup.at[pl.ds(vrow, 128), pl.ds(vcol, 128)],
            wv.at[z, c, pl.ds(vrow, 128), :],
            ld.at[3],
        ),
        pltpu.make_async_copy(keys_h, keys, ld.at[4]),
        pltpu.make_async_copy(rope_h, rope, ld.at[5]),
        pltpu.make_async_copy(vals_h, vals, ld.at[6]),
        pltpu.make_async_copy(cache_h, cache, ld.at[7]),
    ]
    for load in loads:
        load.start()

    barrier = pltpu.get_barrier_semaphore()

    def greet(dev):
        pl.semaphore_signal(barrier, inc=1, device_id=dev, device_id_type=MESH)

    each(1, NZ, lambda k: greet(to_z(k)))
    each(1, NY, lambda k: greet(to_y(k)))
    each(1, NX, lambda k: greet(to_x(k)))
    greet(twin)

    loads[1].wait()

    def permute(i, _):
        rows = pl.ds(pl.multiple_of(i * 256, 256), 256)
        w = wuq_v[rows, :]
        wp[rows, 0:128] = w[:, 0:128]
        wp[rows, 128:256] = w[:, 192:320]
        wp[rows, 256:384] = jnp.concatenate([w[:, 128:192], w[:, 320:384]], axis=1)
        return 0

    lax.fori_loop(0, QL // 256, permute, 0)
    loads[0].wait()
    loads[2].wait()
    loads[3].wait()
    pl.semaphore_wait(barrier, NZ + NY + NX - 2)

    def place(h, up):
        return (zat(-h), h) if up else (zat(h), NZ - h)

    def ring(h, up, view, ss, rs):
        zs, _ = place(h - 1, up)
        k = h if up else NZ - h
        return copy(view(zs), view(zs), ss.at[k], rs.at[k], to_z(1 if up else NZ - 1))

    def ag_view(zs):
        return ag.at[y, zs]

    def wk_view(zs):
        return wk.at[zs, pl.ds(vcol, 128), :]

    def wv_view(zs):
        return wv.at[zs, c, pl.ds(vrow, 128), :]

    tables = ((ag_view, agz_s, agz_r, 4, 3), (wk_view, kz_s, kz_r, 3, 4), (wv_view, vz_s, vz_r, 4, 3))

    def beside(k, up):
        block = ag.at[y, zat(-k)]
        if up:
            return copy(block, block, yp_s.at[k], yp_r.at[k], to_y(1))
        return copy(block, block, ym_s.at[k], ym_r.at[k], to_y(3))

    def hop(h, table):
        view, ss, rs, far_up, far_down = table
        for up, far in ((True, far_up), (False, far_down)):
            if h > 1 and h - 1 <= far:
                zs, k = place(h - 1, up)
                landed(view(zs), ss.at[k], rs.at[k])
            if h <= far:
                one = ring(h, up, view, ss, rs)
                one.start()
                sends.append(one.wait_send)
            if view is ag_view and h - 1 <= far and (h > 1 or up):
                _, k = place(h - 1, up)
                k %= NZ
                beside(k, True).start()
                beside(k, False).start()

    sends.append(lambda: each(0, NZ, lambda k: beside(k, True).wait_send()))
    sends.append(lambda: each(0, NZ, lambda k: beside(k, False).wait_send()))

    def relay(k, up):
        block = ag.at[yat(-1 if up else 1), zat(-k)]
        return copy(block, block, f_s.at[k], f_r.at[k], to_y(1 if up else 3))

    def rows_beside(k, up):
        zs = zat(-k)
        landed(ag.at[yat(-1), zs], yp_s.at[k], yp_r.at[k])
        landed(ag.at[yat(1), zs], ym_s.at[k], ym_r.at[k])
        relay(k, up).start()

    def pair(k):
        rows_beside(k, False)
        rows_beside(NZ - k, True)

    sends.append(lambda: each(0, NZ, lambda k: relay(k, True).wait_send()))

    for h in range(1, 6):
        for table in tables:
            hop(h, table)
        if h == 2:
            rows_beside(0, True)
        elif h > 2:
            pair(h - 2)

    half = wk.at[:, pl.ds(vcol, 128), :]
    push(half, half, kc_s.at[0], kc_r.at[0], twin)

    def wv_x(k):
        block = wv.at[:, c, pl.ds(vrow, 128), :]
        return copy(block, block, vx_s.at[k], vx_r.at[k], to_x(k))

    push_x(wv_x)

    def queries(k):
        yy = yat(k)
        q = nn(ag[yy].reshape(NZ * RQ, QL), wp[...]).astype(BF16)
        qb[yy] = q.reshape(NZ, RQ, 384)
        zq[z, yy] = qb[yy, z]
        push_near(
            lambda j: copy(
                qb.at[yy, zat(j)], zq.at[z, yy], qz_s.at[k, j], qz_r.at[k, j], to_z(j)
            )
        )

    queries(0)
    rows_beside(NZ // 2, False)
    queries(1)
    queries(3)

    live = plen[0]

    def prefix(k, h):
        yy = yat(k)
        hc = slice(h * 128, (h + 1) * 128)
        q = qb[yy].reshape(NZ * RQ, 384)
        qn = q[:, hc]
        qr = q[:, 256 + h * ROPE : 256 + (h + 1) * ROPE]

        def score(t, m):
            t0 = pl.multiple_of(t * TB, TB)
            s = nt(qn, keys[pl.ds(t0, TB), hc]) + nn(qr, rope[:, pl.ds(t0, TB)])
            col = t0 + lax.broadcasted_iota(jnp.int32, s.shape, 1)
            s = jnp.where(col < live, s * SCALE2, -jnp.inf)
            sc[:, pl.ds(t0, TB)] = s
            for j in range(TB // 128):
                m = jnp.maximum(m, s[:, j * 128 : (j + 1) * 128])
            return m

        m = lax.fori_loop(0, PREFIX // TB, score, jnp.full((128, 128), -jnp.inf, F32))
        top = jnp.max(m, axis=1, keepdims=True)

        def weigh(t, carry):
            acc, den = carry
            t0 = pl.multiple_of(t * TB, TB)
            p = jnp.exp2(sc[:, pl.ds(t0, TB)] - top)
            for j in range(TB // 128):
                den = den + p[:, j * 128 : (j + 1) * 128]
            return acc + nn(p.astype(BF16), vals[pl.ds(t0, TB), hc]), den

        zero = jnp.zeros((128, 128), F32)
        acc, den = lax.fori_loop(0, PREFIX // TB, weigh, (zero, zero))
        den = jnp.sum(den, axis=1, keepdims=True)
        po[h, yy] = (acc / den).reshape(NZ, RQ, VD)
        lse2 = jnp.broadcast_to(top + jnp.log(den) * math.log2(math.e), (128, 128))
        plse[h, yy] = lse2.reshape(NZ, RQ, 128)

    loads[4].wait()
    loads[5].wait()
    loads[6].wait()
    prefix(0, 0)

    each(0, NZ, lambda k: landed(ag.at[yat(2), zat(-k)], f_s.at[k], f_r.at[k]))
    queries(2)

    prefix(0, 1)

    def arrive(k):
        each(1, NZ, lambda j: landed(zq.at[zat(-j), yat(k)], qz_s.at[k, j], qz_r.at[k, j]))

    def absorb(ks):
        def one(zz, _):
            q = jnp.concatenate([zq[zz, yat(k)] for k in ks], axis=0)
            rows = pl.ds(pl.multiple_of(zz * RQ, RQ), RQ)
            a = [nn(q[:, h * 128 : (h + 1) * 128], wk[zz, h * 128 : (h + 1) * 128, :]) for h in range(2)]
            for i, k in enumerate(ks):
                for t in range(2):
                    part = slice(i * RQ + t * RH, i * RQ + (t + 1) * RH)
                    both = jnp.concatenate([a[0][part], a[1][part]], axis=0)
                    absb[t, yat(k), rows, :] = both.astype(BF16)
                rps[yat(k), rows, :] = q[i * RQ : (i + 1) * RQ, 256:384]
            return 0

        lax.fori_loop(0, NZ, one, 0)

    def send_absorbed(t, k):
        push(absb.at[t, yat(k)], rec1.at[t, y], a_s.at[t, k], a_r.at[t, k], to_y(k))

    def send_rotary(k):
        push(rps.at[yat(k)], rec1r.at[y], ar_s.at[k], ar_r.at[k], to_y(k))

    arrive(1)
    arrive(3)
    landed(wk.at[:, pl.ds(ccol, 128), :], kc_s.at[0], kc_r.at[0])
    absorb((1, 3))
    for k in (1, 3):
        send_rotary(k)
        send_absorbed(0, k)
    arrive(0)
    arrive(2)
    absorb((2, 0))
    send_rotary(2)
    send_absorbed(0, 2)
    for k in (1, 3, 2):
        send_absorbed(1, k)

    def spread(t, k, src):
        rows = pl.ds(pl.multiple_of(yat(k) * 128, 128), 128)
        for j in range(4):
            qf[t, j, rows, :] = src[:, j * 128 : (j + 1) * 128].astype(F32)

    def spread_rotary(k, src):
        base = yat(k) * 128
        for zz in range(NZ):
            tile = src[zz * RQ : (zz + 1) * RQ, :].astype(F32)
            for h in range(2):
                part = tile[:, h * ROPE : (h + 1) * ROPE]
                rows = pl.ds(pl.multiple_of(base + (zz * 2 + h) * RH, RH), RH)
                for t in range(2):
                    qrf[t, rows, 0:ROPE] = part[t * RH : (t + 1) * RH]

    spread_rotary(0, rps.at[y])
    spread(0, 0, absb.at[0, y])
    spread(1, 0, absb.at[1, y])
    prefix(1, 0)
    prefix(1, 1)

    def wv_landed(k):
        rows = pl.ds(pl.multiple_of(lax.rem(x - k + NX, NX) * 128, 128), 128)
        landed(wv.at[:, c, rows, :], vx_s.at[k], vx_r.at[k])

    each(1, NX, wv_landed)
    half = wv.at[:, c]
    push(half, half, vc_s.at[0], vc_r.at[0], twin)

    lse[...] = jnp.zeros_like(lse)
    loads[7].wait()
    for k in range(1, NY):
        yy = yat(-k)
        landed(rec1r.at[yy], ar_s.at[k], ar_r.at[k])
        spread_rotary(-k, rec1r.at[yy])

    def attend(t):
        for k in range(1, NY):
            yy = yat(-k)
            landed(rec1.at[t, yy], a_s.at[t, k], a_r.at[t, k])
            spread(t, -k, rec1.at[t, yy])

        def private(i, _):
            r = t * RH + i
            mine = pl.ds(i, 64, stride=RH)
            q = jnp.concatenate([qf[t, j, mine, :] for j in range(4)], axis=1).astype(BF16)
            qr = qrf[t, mine, :][:, :ROPE].astype(BF16)
            s = nn(q, cache[r, :KVL, :]) + nn(qr, cache[r, KVL:, :])
            col = lax.broadcasted_iota(jnp.int32, s.shape, 1)
            s = jnp.where(col < lens[r], s * SCALE2, -jnp.inf)
            top = jnp.max(s, axis=1, keepdims=True)
            p = jnp.exp2(s - top)
            den = jnp.sum(p, axis=1, keepdims=True)
            latent = nt(p.astype(BF16), cache[r, :KVL, :]) / den
            for j in range(4):
                lf[j, mine, :] = latent[:, j * 128 : (j + 1) * 128]
            lse2 = (top + jnp.log(den) * math.log2(math.e)).reshape(NY, 16, 1)
            lane = lax.broadcasted_iota(jnp.int32, lse.shape[1:], 2)
            lse[t] = jnp.where(lane == r, lse2, lse[t])
            return 0

        lax.fori_loop(0, RH, private, 0, unroll=2)

        def gather(k, dst):
            rows = pl.ds(pl.multiple_of(yat(k) * 128, 128), 128)
            for j in range(4):
                dst[:, j * 128 : (j + 1) * 128] = lf[j, rows, :].astype(BF16)

        for k in (2, 1, 3):
            yy = yat(k)
            gather(k, send2.at[t, yy])
            push(lse.at[t, yy], recl.at[t, y], bl_s.at[t, k], bl_r.at[t, k], to_y(k))
            push(send2.at[t, yy], rec2.at[t, y], b_s.at[t, k], b_r.at[t, k], to_y(k))
        gather(0, rec2.at[t, y])
        recl[t, y] = lse[t, y]

    attend(0)
    attend(1)
    prefix(3, 0)
    landed(wv.at[:, 1 - c], vc_s.at[0], vc_r.at[0])
    mbuf[...] = jnp.zeros_like(mbuf)

    def deliver(t):
        for k in range(1, NY):
            landed(recl.at[t, yat(-k)], bl_s.at[t, k], bl_r.at[t, k])
        total = recl[t, 0]
        for yy in range(1, NY):
            total = total + pltpu.roll(recl[t, yy], yy * RQ, 1)
        for zz in range(NZ):
            mbuf[t, zz, 0:2] = total[2 * zz : 2 * zz + 2]
        recm[t, z] = mbuf[t, z]
        push_near(lambda k: copy(mbuf.at[t, zat(k)], recm.at[t, z], cm_s.at[t, k], cm_r.at[t, k], to_z(k)))
        for k in range(1, NY):
            landed(rec2.at[t, yat(-k)], b_s.at[t, k], b_r.at[t, k])

        def project(zz, dst):
            rows = pl.ds(pl.multiple_of(zz * RQ, RQ), RQ)
            lat = jnp.concatenate([rec2[t, yy, rows, :] for yy in range(NY)], axis=0)
            for h in range(2):
                o = nn(lat, wv[zz, h]).reshape(NY, 2, RH, VD)[:, h].reshape(NY * RH, VD)
                dst[t, zz, h] = o.astype(BF16)

        def heads(k):
            return copy(outz.at[t, zat(k)], recz.at[t, z], c_s.at[t, k], c_r.at[t, k], to_z(k))

        def give(i):
            k = near(NZ - i)
            project(zat(k), outz)
            heads(k).start()

        each(1, NZ, give)
        sends.append(lambda: each(1, NZ, lambda k: heads(k).wait_send()))
        project(z, recz)

    deliver(0)
    prefix(3, 1)
    deliver(1)
    prefix(2, 0)
    prefix(2, 1)

    def merge(t, zz, h):
        diag = (
            lax.broadcasted_iota(jnp.int32, (NY, RH, 128), 0) * RQ
            + lax.broadcasted_iota(jnp.int32, (NY, RH, 128), 1)
            + t * RH
        ) == lax.broadcasted_iota(jnp.int32, (NY, RH, 128), 2)
        row = recm[t, zz, h : h + 1, :].reshape(1, 1, 128)
        plane = jnp.sum(jnp.where(diag, row, 0.0), axis=2, keepdims=True)
        part = slice(t * RH, (t + 1) * RH)
        mine = po[h, :, zz, part, :]
        mine_lse = plse[h, :, zz, part, :]
        upper = jnp.maximum(mine_lse, plane)
        first = jnp.exp2(mine_lse - upper)
        second = jnp.exp2(plane - upper)
        theirs = recz[t, zz, h].astype(F32).reshape(NY, RH, VD)
        return (first * mine + second * theirs) / (first + second)

    def early(zz):
        for h in range(2):
            half0[zz, h] = merge(0, zz, h)

    def late(zz):
        for h in range(2):
            both = jnp.concatenate([half0[zz, h], merge(1, zz, h)], axis=1).astype(BF16)
            for yy in range(NY):
                rows = pl.ds(pl.multiple_of(yy * 128 + zz * RQ, RQ), RQ)
                out[rows, h * 128 : (h + 1) * 128] = both[yy]

    def finish(t, step):
        def one(i):
            k = near(i)
            zz = zat(-k)
            landed(recm.at[t, zz], cm_s.at[t, k], cm_r.at[t, k])
            landed(recz.at[t, zz], c_s.at[t, k], c_r.at[t, k])
            step(zz)

        step(z)
        each(1, NZ, one)

    finish(0, early)
    finish(1, late)
    for wait in sends:
        wait()


def body(
    q_latent,
    w_uq,
    w_kup,
    w_vup,
    prefix_keys,
    prefix_values,
    prefix_rope,
    private_cache,
    lengths,
    prefix_len,
):
    cache = jnp.transpose(private_cache, (0, 2, 1))
    vm = pltpu.VMEM
    dma = pltpu.SemaphoreType.DMA
    hbm = pl.BlockSpec(memory_space=pl.ANY)
    smem = pl.BlockSpec(memory_space=pltpu.SMEM)
    scratch = [
        vm((QL, 384), BF16),
        vm((QL, 384), BF16),
        vm((PREFIX, 256), BF16),
        vm((PREFIX, 256), BF16),
        vm((ROPE, PREFIX), BF16),
        vm((RQ, KVL + ROPE, SLOTS), BF16),
        vm((NY, NZ, RQ, QL), BF16),
        vm((NY, NZ, RQ, 384), BF16),
        vm((NZ, NY, RQ, 384), BF16),
        vm((NZ, 256, KVL), BF16),
        vm((NZ, 2, KVL, VD), BF16),
        vm((2, NY, 128, KVL), BF16),
        vm((NY, NZ * RQ, 128), BF16),
        vm((2, NY, 128, KVL), BF16),
        vm((NY, NZ * RQ, 128), BF16),
        vm((2, 4, 512, 128), F32),
        vm((2, 512, 128), F32),
        vm((4, 512, 128), F32),
        vm((2, NY, 16, 128), F32),
        vm((2, NY, 128, KVL), BF16),
        vm((2, NY, 128, KVL), BF16),
        vm((2, NY, 16, 128), F32),
        vm((2, NZ, 2, NY * RH, VD), BF16),
        vm((2, NZ, 8, 128), F32),
        vm((2, NZ, 2, NY * RH, VD), BF16),
        vm((2, NZ, 8, 128), F32),
        vm((NZ, 2, NY, RH, VD), F32),
        vm((128, PREFIX), F32),
        vm((2, NY, NZ, RQ, VD), F32),
        vm((2, NY, NZ, RQ, 128), F32),
        dma((8,)),
    ]
    sems = [8, 8, 8, 8, 8, 8, 8, 8, (4, 8), (4, 8), 8, 8, 1, 1, 8, 8, 4, 4, 1, 1]
    sems += [(2, 4), (2, 4), 4, 4] + [(2, 4)] * 4 + [(2, 8)] * 4
    scratch += [dma(n if isinstance(n, tuple) else (n,)) for n in sems]
    return pl.pallas_call(
        kernel,
        out_shape=jax.ShapeDtypeStruct((512, 256), BF16),
        in_specs=[hbm] * 8 + [smem] * 2,
        out_specs=pl.BlockSpec(memory_space=vm),
        scratch_shapes=scratch,
        compiler_params=pltpu.CompilerParams(
            collective_id=0, has_side_effects=True, vmem_limit_bytes=58 * 2**20
        ),
        cost_estimate=pl.CostEstimate(
            flops=5 * 10**9, bytes_accessed=14 * 10**6, transcendentals=5 * 10**6
        ),
        name="latent_attention",
    )(
        q_latent, w_uq, w_kup, w_vup, prefix_keys, prefix_values, prefix_rope, cache, lengths,
        prefix_len,
    )


def solution(mesh):
    placed = (
        P(("grp", "dev"), None),
        P(None, "dev"),
        P("dev", None),
        P(None, "dev"),
        P("grp", "dev"),
        P("grp", "dev"),
        P(None, "grp"),
        P(("grp", "dev"), None, None),
        P(("grp", "dev")),
        P("grp"),
    )
    return jax.shard_map(
        body, mesh=mesh, in_specs=placed, out_specs=P("grp", "dev"), check_vma=False
    )
```

```python
import math

import jax
import jax.numpy as jnp
from jax import lax
from jax.experimental import pallas as pl
from jax.experimental.pallas import tpu as pltpu
from jax.sharding import PartitionSpec as P

KVL = 512
NOPE = 128
ROPE = 64
VD = 128
MESH = pl.DeviceIdType.MESH
NY, NZ, NX = 4, 8, 4
RQ = 16
RH = 8
SLOTS = 384
PREFIX = 4096
QL = 1536
TB = 2048
SCALE2 = math.log2(math.e) / math.sqrt(NOPE + ROPE)
F32 = jnp.float32
BF16 = jnp.bfloat16


def nn(a, b):
    return lax.dot_general(a, b, (((1,), (0,)), ((), ())), preferred_element_type=F32)


def nt(a, b):
    return lax.dot_general(a, b, (((1,), (1,)), ((), ())), preferred_element_type=F32)


def near(i):
    odd = lax.rem(i, 2)
    return odd * lax.div(i + 1, 2) + (1 - odd) * (NZ - lax.div(i, 2))


def each(low, high, step):
    def one(i, carry):
        step(i)
        return carry

    lax.fori_loop(low, high, one, 0)


def kernel(
    ql, wuq, wkup, wvup, keys_h, vals_h, rope_h, cache_h, lens, plen, out,
    wuq_v, wp, keys, vals, rope, cache, ag, qb, zq, wk, wv, absb, rps, rec1, rec1r,
    qf, qrf, lf, lse, send2, rec2, recl, outz, mbuf, recz, recm, half0, sc, po, plse,
    ld, agz_s, agz_r, yp_s, yp_r, ym_s, ym_r, f_s, f_r, qz_s, qz_r,
    kz_s, kz_r, kc_s, kc_r, vz_s, vz_r, vx_s, vx_r, vc_s, vc_r,
    a_s, a_r, ar_s, ar_r, b_s, b_r, bl_s, bl_r, c_s, c_r, cm_s, cm_r,
):
    g = lax.axis_index("grp")
    d = lax.axis_index("dev")
    x, c = lax.div(g, 2), lax.rem(g, 2)
    y, z = lax.div(d, NZ), lax.rem(d, NZ)

    def yat(k):
        return lax.rem(y + (k + NY), NY)

    def zat(k):
        return lax.rem(z + (k + NZ), NZ)

    def to_y(k):
        return (g, yat(k) * NZ + z)

    def to_z(k):
        return (g, y * NZ + zat(k))

    def to_x(k):
        return (lax.rem(x + k, NX) * 2 + c, d)

    twin = (x * 2 + 1 - c, d)
    sends = []

    def copy(src, dst, ss, rs, dev):
        return pltpu.make_async_remote_copy(
            src_ref=src, dst_ref=dst, send_sem=ss, recv_sem=rs, device_id=dev, device_id_type=MESH
        )

    def push(*what):
        one = copy(*what)
        one.start()
        sends.append(one.wait_send)

    def push_near(what):
        each(1, NZ, lambda i: what(near(i)).start())
        sends.append(lambda: each(1, NZ, lambda i: what(i).wait_send()))

    def push_x(what):
        each(1, NX, lambda i: what(i).start())
        sends.append(lambda: each(1, NX, lambda i: what(i).wait_send()))

    def landed(dst, ss, rs):
        pltpu.make_async_remote_copy(
            src_ref=dst, dst_ref=dst, send_sem=ss, recv_sem=rs, device_id=twin, device_id_type=MESH
        ).wait_recv()

    vrow = pl.multiple_of(x * 128, 128)
    vcol = pl.multiple_of(c * 128, 128)
    ccol = pl.multiple_of((1 - c) * 128, 128)

    loads = [
        pltpu.make_async_copy(ql, ag.at[y, z], ld.at[0]),
        pltpu.make_async_copy(wuq, wuq_v, ld.at[1]),
        pltpu.make_async_copy(wkup.at[pl.ds(vcol, 128), :], wk.at[z, pl.ds(vcol, 128), :], ld.at[2]),
        pltpu.make_async_copy(
            wvup.at[pl.ds(vrow, 128), pl.ds(vcol, 128)],
            wv.at[z, c, pl.ds(vrow, 128), :],
            ld.at[3],
        ),
        pltpu.make_async_copy(keys_h, keys, ld.at[4]),
        pltpu.make_async_copy(rope_h, rope, ld.at[5]),
        pltpu.make_async_copy(vals_h, vals, ld.at[6]),
        pltpu.make_async_copy(cache_h, cache, ld.at[7]),
    ]
    for load in loads:
        load.start()

    barrier = pltpu.get_barrier_semaphore()

    def greet(dev):
        pl.semaphore_signal(barrier, inc=1, device_id=dev, device_id_type=MESH)

    each(1, NZ, lambda k: greet(to_z(k)))
    each(1, NY, lambda k: greet(to_y(k)))
    each(1, NX, lambda k: greet(to_x(k)))
    greet(twin)

    loads[1].wait()

    def permute(i, _):
        rows = pl.ds(pl.multiple_of(i * 256, 256), 256)
        w = wuq_v[rows, :]
        wp[rows, 0:128] = w[:, 0:128]
        wp[rows, 128:256] = w[:, 192:320]
        wp[rows, 256:384] = jnp.concatenate([w[:, 128:192], w[:, 320:384]], axis=1)
        return 0

    lax.fori_loop(0, QL // 256, permute, 0)
    loads[0].wait()
    loads[2].wait()
    loads[3].wait()
    pl.semaphore_wait(barrier, NZ + NY + NX - 2)

    def place(h, up):
        return (zat(-h), h) if up else (zat(h), NZ - h)

    def ring(h, up, view, ss, rs):
        zs, _ = place(h - 1, up)
        k = h if up else NZ - h
        return copy(view(zs), view(zs), ss.at[k], rs.at[k], to_z(1 if up else NZ - 1))

    def ag_view(zs):
        return ag.at[y, zs]

    def wk_view(zs):
        return wk.at[zs, pl.ds(vcol, 128), :]

    def wv_view(zs):
        return wv.at[zs, c, pl.ds(vrow, 128), :]

    tables = ((ag_view, agz_s, agz_r, 4, 3), (wk_view, kz_s, kz_r, 3, 4), (wv_view, vz_s, vz_r, 4, 3))

    def beside(k, up):
        block = ag.at[y, zat(-k)]
        if up:
            return copy(block, block, yp_s.at[k], yp_r.at[k], to_y(1))
        return copy(block, block, ym_s.at[k], ym_r.at[k], to_y(3))

    def hop(h, table):
        view, ss, rs, far_up, far_down = table
        for up, far in ((True, far_up), (False, far_down)):
            if h > 1 and h - 1 <= far:
                zs, k = place(h - 1, up)
                landed(view(zs), ss.at[k], rs.at[k])
            if h <= far:
                one = ring(h, up, view, ss, rs)
                one.start()
                sends.append(one.wait_send)
            if view is ag_view and h - 1 <= far and (h > 1 or up):
                _, k = place(h - 1, up)
                k %= NZ
                beside(k, True).start()
                beside(k, False).start()

    sends.append(lambda: each(0, NZ, lambda k: beside(k, True).wait_send()))
    sends.append(lambda: each(0, NZ, lambda k: beside(k, False).wait_send()))

    def relay(k, up):
        block = ag.at[yat(-1 if up else 1), zat(-k)]
        return copy(block, block, f_s.at[k], f_r.at[k], to_y(1 if up else 3))

    def rows_beside(k, up):
        zs = zat(-k)
        landed(ag.at[yat(-1), zs], yp_s.at[k], yp_r.at[k])
        landed(ag.at[yat(1), zs], ym_s.at[k], ym_r.at[k])
        relay(k, up).start()

    def pair(k):
        rows_beside(k, False)
        rows_beside(NZ - k, True)

    sends.append(lambda: each(0, NZ, lambda k: relay(k, True).wait_send()))

    for h in range(1, 6):
        for table in tables:
            hop(h, table)
        if h == 2:
            rows_beside(0, True)
        elif h > 2:
            pair(h - 2)

    half = wk.at[:, pl.ds(vcol, 128), :]
    push(half, half, kc_s.at[0], kc_r.at[0], twin)

    def wv_x(k):
        block = wv.at[:, c, pl.ds(vrow, 128), :]
        return copy(block, block, vx_s.at[k], vx_r.at[k], to_x(k))

    push_x(wv_x)

    def queries(k):
        yy = yat(k)
        q = nn(ag[yy].reshape(NZ * RQ, QL), wp[...]).astype(BF16)
        qb[yy] = q.reshape(NZ, RQ, 384)
        zq[z, yy] = qb[yy, z]
        push_near(
            lambda j: copy(
                qb.at[yy, zat(j)], zq.at[z, yy], qz_s.at[k, j], qz_r.at[k, j], to_z(j)
            )
        )

    queries(0)
    rows_beside(NZ // 2, False)
    queries(1)
    queries(3)

    live = plen[0]

    def prefix(ks, h):
        hc = slice(h * 128, (h + 1) * 128)
        q = jnp.concatenate([qb[yat(k)].reshape(NZ * RQ, 384) for k in ks], axis=0)
        n = q.shape[0]
        qn = q[:, hc]
        qr = q[:, 256 + h * ROPE : 256 + (h + 1) * ROPE]

        def score(t, m):
            t0 = pl.multiple_of(t * TB, TB)
            s = nt(qn, keys[pl.ds(t0, TB), hc]) + nn(qr, rope[:, pl.ds(t0, TB)])
            col = t0 + lax.broadcasted_iota(jnp.int32, s.shape, 1)
            s = jnp.where(col < live, s * SCALE2, -jnp.inf)
            sc[:, pl.ds(t0, TB)] = s
            for j in range(TB // 128):
                m = jnp.maximum(m, s[:, j * 128 : (j + 1) * 128])
            return m

        m = lax.fori_loop(0, PREFIX // TB, score, jnp.full((n, 128), -jnp.inf, F32))
        top = jnp.max(m, axis=1, keepdims=True)

        def weigh(t, carry):
            acc, den = carry
            t0 = pl.multiple_of(t * TB, TB)
            p = jnp.exp2(sc[:, pl.ds(t0, TB)] - top)
            for j in range(TB // 128):
                den = den + p[:, j * 128 : (j + 1) * 128]
            return acc + nn(p.astype(BF16), vals[pl.ds(t0, TB), hc]), den

        zero = jnp.zeros((n, 128), F32)
        acc, den = lax.fori_loop(0, PREFIX // TB, weigh, (zero, zero))
        den = jnp.sum(den, axis=1, keepdims=True)
        mean = acc / den
        lse2 = jnp.broadcast_to(top + jnp.log(den) * math.log2(math.e), (n, 128))
        for i, k in enumerate(ks):
            part = slice(i * 128, (i + 1) * 128)
            po[h, yat(k)] = mean[part].reshape(NZ, RQ, VD)
            plse[h, yat(k)] = lse2[part].reshape(NZ, RQ, 128)

    loads[4].wait()
    loads[5].wait()
    loads[6].wait()
    prefix((0, 1), 0)

    each(0, NZ, lambda k: landed(ag.at[yat(2), zat(-k)], f_s.at[k], f_r.at[k]))
    queries(2)


    def arrive(k):
        each(1, NZ, lambda j: landed(zq.at[zat(-j), yat(k)], qz_s.at[k, j], qz_r.at[k, j]))

    def absorb(ks):
        def one(zz, _):
            q = jnp.concatenate([zq[zz, yat(k)] for k in ks], axis=0)
            rows = pl.ds(pl.multiple_of(zz * RQ, RQ), RQ)
            a = [nn(q[:, h * 128 : (h + 1) * 128], wk[zz, h * 128 : (h + 1) * 128, :]) for h in range(2)]
            for i, k in enumerate(ks):
                for t in range(2):
                    part = slice(i * RQ + t * RH, i * RQ + (t + 1) * RH)
                    both = jnp.concatenate([a[0][part], a[1][part]], axis=0)
                    absb[t, yat(k), rows, :] = both.astype(BF16)
                rps[yat(k), rows, :] = q[i * RQ : (i + 1) * RQ, 256:384]
            return 0

        lax.fori_loop(0, NZ, one, 0)

    def send_absorbed(t, k):
        push(absb.at[t, yat(k)], rec1.at[t, y], a_s.at[t, k], a_r.at[t, k], to_y(k))

    def send_rotary(k):
        push(rps.at[yat(k)], rec1r.at[y], ar_s.at[k], ar_r.at[k], to_y(k))

    arrive(1)
    arrive(3)
    landed(wk.at[:, pl.ds(ccol, 128), :], kc_s.at[0], kc_r.at[0])
    absorb((1, 3))
    for k in (1, 3):
        send_rotary(k)
        send_absorbed(0, k)
    arrive(0)
    arrive(2)
    absorb((2, 0))
    send_rotary(2)
    send_absorbed(0, 2)
    for k in (1, 3, 2):
        send_absorbed(1, k)

    def spread(t, k, src):
        rows = pl.ds(pl.multiple_of(yat(k) * 128, 128), 128)
        for j in range(4):
            qf[t, j, rows, :] = src[:, j * 128 : (j + 1) * 128].astype(F32)

    def spread_rotary(k, src):
        base = yat(k) * 128
        for zz in range(NZ):
            tile = src[zz * RQ : (zz + 1) * RQ, :].astype(F32)
            for h in range(2):
                part = tile[:, h * ROPE : (h + 1) * ROPE]
                rows = pl.ds(pl.multiple_of(base + (zz * 2 + h) * RH, RH), RH)
                for t in range(2):
                    qrf[t, rows, 0:ROPE] = part[t * RH : (t + 1) * RH]

    spread_rotary(0, rps.at[y])
    spread(0, 0, absb.at[0, y])
    spread(1, 0, absb.at[1, y])
    prefix((0, 1), 1)
    prefix((3, 2), 0)

    def wv_landed(k):
        rows = pl.ds(pl.multiple_of(lax.rem(x - k + NX, NX) * 128, 128), 128)
        landed(wv.at[:, c, rows, :], vx_s.at[k], vx_r.at[k])

    each(1, NX, wv_landed)
    half = wv.at[:, c]
    push(half, half, vc_s.at[0], vc_r.at[0], twin)

    lse[...] = jnp.zeros_like(lse)
    loads[7].wait()
    for k in range(1, NY):
        yy = yat(-k)
        landed(rec1r.at[yy], ar_s.at[k], ar_r.at[k])
        spread_rotary(-k, rec1r.at[yy])

    def attend(t):
        for k in range(1, NY):
            yy = yat(-k)
            landed(rec1.at[t, yy], a_s.at[t, k], a_r.at[t, k])
            spread(t, -k, rec1.at[t, yy])

        def private(i, _):
            r = t * RH + i
            mine = pl.ds(i, 64, stride=RH)
            q = jnp.concatenate([qf[t, j, mine, :] for j in range(4)], axis=1).astype(BF16)
            qr = qrf[t, mine, :][:, :ROPE].astype(BF16)
            s = nn(q, cache[r, :KVL, :]) + nn(qr, cache[r, KVL:, :])
            col = lax.broadcasted_iota(jnp.int32, s.shape, 1)
            s = jnp.where(col < lens[r], s * SCALE2, -jnp.inf)
            top = jnp.max(s, axis=1, keepdims=True)
            p = jnp.exp2(s - top)
            den = jnp.sum(p, axis=1, keepdims=True)
            latent = nt(p.astype(BF16), cache[r, :KVL, :]) / den
            for j in range(4):
                lf[j, mine, :] = latent[:, j * 128 : (j + 1) * 128]
            lse2 = (top + jnp.log(den) * math.log2(math.e)).reshape(NY, 16, 1)
            lane = lax.broadcasted_iota(jnp.int32, lse.shape[1:], 2)
            lse[t] = jnp.where(lane == r, lse2, lse[t])
            return 0

        lax.fori_loop(0, RH, private, 0, unroll=2)

        def gather(k, dst):
            rows = pl.ds(pl.multiple_of(yat(k) * 128, 128), 128)
            for j in range(4):
                dst[:, j * 128 : (j + 1) * 128] = lf[j, rows, :].astype(BF16)

        for k in (2, 1, 3):
            yy = yat(k)
            gather(k, send2.at[t, yy])
            push(lse.at[t, yy], recl.at[t, y], bl_s.at[t, k], bl_r.at[t, k], to_y(k))
            push(send2.at[t, yy], rec2.at[t, y], b_s.at[t, k], b_r.at[t, k], to_y(k))
        gather(0, rec2.at[t, y])
        recl[t, y] = lse[t, y]

    attend(0)
    attend(1)
    prefix((3, 2), 1)
    landed(wv.at[:, 1 - c], vc_s.at[0], vc_r.at[0])
    mbuf[...] = jnp.zeros_like(mbuf)

    def deliver(t):
        for k in range(1, NY):
            landed(recl.at[t, yat(-k)], bl_s.at[t, k], bl_r.at[t, k])
        total = recl[t, 0]
        for yy in range(1, NY):
            total = total + pltpu.roll(recl[t, yy], yy * RQ, 1)
        for zz in range(NZ):
            mbuf[t, zz, 0:2] = total[2 * zz : 2 * zz + 2]
        recm[t, z] = mbuf[t, z]
        push_near(lambda k: copy(mbuf.at[t, zat(k)], recm.at[t, z], cm_s.at[t, k], cm_r.at[t, k], to_z(k)))
        for k in range(1, NY):
            landed(rec2.at[t, yat(-k)], b_s.at[t, k], b_r.at[t, k])

        def project(zz, dst):
            rows = pl.ds(pl.multiple_of(zz * RQ, RQ), RQ)
            lat = jnp.concatenate([rec2[t, yy, rows, :] for yy in range(NY)], axis=0)
            for h in range(2):
                o = nn(lat, wv[zz, h]).reshape(NY, 2, RH, VD)[:, h].reshape(NY * RH, VD)
                dst[t, zz, h] = o.astype(BF16)

        def heads(k):
            return copy(outz.at[t, zat(k)], recz.at[t, z], c_s.at[t, k], c_r.at[t, k], to_z(k))

        def give(i):
            k = near(NZ - i)
            project(zat(k), outz)
            heads(k).start()

        each(1, NZ, give)
        sends.append(lambda: each(1, NZ, lambda k: heads(k).wait_send()))
        project(z, recz)

    deliver(0)
    deliver(1)

    def merge(t, zz, h):
        diag = (
            lax.broadcasted_iota(jnp.int32, (NY, RH, 128), 0) * RQ
            + lax.broadcasted_iota(jnp.int32, (NY, RH, 128), 1)
            + t * RH
        ) == lax.broadcasted_iota(jnp.int32, (NY, RH, 128), 2)
        row = recm[t, zz, h : h + 1, :].reshape(1, 1, 128)
        plane = jnp.sum(jnp.where(diag, row, 0.0), axis=2, keepdims=True)
        part = slice(t * RH, (t + 1) * RH)
        mine = po[h, :, zz, part, :]
        mine_lse = plse[h, :, zz, part, :]
        upper = jnp.maximum(mine_lse, plane)
        first = jnp.exp2(mine_lse - upper)
        second = jnp.exp2(plane - upper)
        theirs = recz[t, zz, h].astype(F32).reshape(NY, RH, VD)
        return (first * mine + second * theirs) / (first + second)

    def early(zz):
        for h in range(2):
            half0[zz, h] = merge(0, zz, h)

    def late(zz):
        for h in range(2):
            both = jnp.concatenate([half0[zz, h], merge(1, zz, h)], axis=1).astype(BF16)
            for yy in range(NY):
                rows = pl.ds(pl.multiple_of(yy * 128 + zz * RQ, RQ), RQ)
                out[rows, h * 128 : (h + 1) * 128] = both[yy]

    def finish(t, step):
        def one(i):
            k = near(i)
            zz = zat(-k)
            landed(recm.at[t, zz], cm_s.at[t, k], cm_r.at[t, k])
            landed(recz.at[t, zz], c_s.at[t, k], c_r.at[t, k])
            step(zz)

        step(z)
        each(1, NZ, one)

    finish(0, early)
    finish(1, late)
    for wait in sends:
        wait()


def body(
    q_latent,
    w_uq,
    w_kup,
    w_vup,
    prefix_keys,
    prefix_values,
    prefix_rope,
    private_cache,
    lengths,
    prefix_len,
):
    cache = jnp.transpose(private_cache, (0, 2, 1))
    vm = pltpu.VMEM
    dma = pltpu.SemaphoreType.DMA
    hbm = pl.BlockSpec(memory_space=pl.ANY)
    smem = pl.BlockSpec(memory_space=pltpu.SMEM)
    scratch = [
        vm((QL, 384), BF16),
        vm((QL, 384), BF16),
        vm((PREFIX, 256), BF16),
        vm((PREFIX, 256), BF16),
        vm((ROPE, PREFIX), BF16),
        vm((RQ, KVL + ROPE, SLOTS), BF16),
        vm((NY, NZ, RQ, QL), BF16),
        vm((NY, NZ, RQ, 384), BF16),
        vm((NZ, NY, RQ, 384), BF16),
        vm((NZ, 256, KVL), BF16),
        vm((NZ, 2, KVL, VD), BF16),
        vm((2, NY, 128, KVL), BF16),
        vm((NY, NZ * RQ, 128), BF16),
        vm((2, NY, 128, KVL), BF16),
        vm((NY, NZ * RQ, 128), BF16),
        vm((2, 4, 512, 128), F32),
        vm((2, 512, 128), F32),
        vm((4, 512, 128), F32),
        vm((2, NY, 16, 128), F32),
        vm((2, NY, 128, KVL), BF16),
        vm((2, NY, 128, KVL), BF16),
        vm((2, NY, 16, 128), F32),
        vm((2, NZ, 2, NY * RH, VD), BF16),
        vm((2, NZ, 8, 128), F32),
        vm((2, NZ, 2, NY * RH, VD), BF16),
        vm((2, NZ, 8, 128), F32),
        vm((NZ, 2, NY, RH, VD), F32),
        vm((256, PREFIX), F32),
        vm((2, NY, NZ, RQ, VD), F32),
        vm((2, NY, NZ, RQ, 128), F32),
        dma((8,)),
    ]
    sems = [8, 8, 8, 8, 8, 8, 8, 8, (4, 8), (4, 8), 8, 8, 1, 1, 8, 8, 4, 4, 1, 1]
    sems += [(2, 4), (2, 4), 4, 4] + [(2, 4)] * 4 + [(2, 8)] * 4
    scratch += [dma(n if isinstance(n, tuple) else (n,)) for n in sems]
    return pl.pallas_call(
        kernel,
        out_shape=jax.ShapeDtypeStruct((512, 256), BF16),
        in_specs=[hbm] * 8 + [smem] * 2,
        out_specs=pl.BlockSpec(memory_space=vm),
        scratch_shapes=scratch,
        compiler_params=pltpu.CompilerParams(
            collective_id=0, has_side_effects=True, vmem_limit_bytes=58 * 2**20
        ),
        cost_estimate=pl.CostEstimate(
            flops=5 * 10**9, bytes_accessed=14 * 10**6, transcendentals=5 * 10**6
        ),
        name="latent_attention",
    )(
        q_latent, w_uq, w_kup, w_vup, prefix_keys, prefix_values, prefix_rope, cache, lengths,
        prefix_len,
    )


def solution(mesh):
    placed = (
        P(("grp", "dev"), None),
        P(None, "dev"),
        P("dev", None),
        P(None, "dev"),
        P("grp", "dev"),
        P("grp", "dev"),
        P(None, "grp"),
        P(("grp", "dev"), None, None),
        P(("grp", "dev")),
        P("grp"),
    )
    return jax.shard_map(
        body, mesh=mesh, in_specs=placed, out_specs=P("grp", "dev"), check_vma=False
    )
```
